32 devices in a mesh: row: 4 (over x, core), col: 8 (over z, y).
Axes of the slice: x: 2, y: 2, z: 4, core: 2. Of those that a mesh axis runs over, the one named last changes fastest.
Arguments:
- hamiltonian_blocks: float32 [4, 8, 320, 128, 128], P('row', 'col'), may hold values from -0.0625 to 0.0625
- block_vectors: float32 [16, 32768], P(None, ('row', 'col')), may hold values from -6 to 6
- row_list: int32 [4, 8, 320], P('row', 'col'), may hold values from 0 to 63, as said below
- col_list: int32 [4, 8, 320], P('row', 'col'), may hold values from 0 to 31, as said below
- counts: int32 [4, 8], P('row', 'col'), may hold values from 1 to 320, as said below
Outputs:
- image_vectors: float32 [16, 32768], P(None, ('row', 'col'))
The draws below stay inside these ranges and needn't reach their ends.
Inputs may be any that keep to these rules, and one draw needn't show every extreme that they name: row_list gives a block row within the tile row, at least that of the tile's column block for blocks on the tile's own diagonal segment; every tile has a slot at the last block row. col_list of tile (r, c) names only column blocks of segments with row index at most r, so stored blocks lie on or below the block diagonal; the last tile row reaches the last column block. The live slots of a tile are its first counts slots; tiles of the last tile row are full and the count grows with the tile row.
All inputs are finite; a program needn't handle non-finite values.
Results may differ from the reference program's by a relative error of at most 0.0003.
Values sent between devices are 32-bit elements; how exact they have to be, the bound alone decides.
A program may use at most 128 MiB of HBM per device.

```python
import jax
import jax.numpy as jnp
from jax import lax

BS = 128
K = 16
SB = 8
CAP = 320
NBASIS = 32768
N_ROW = 4
N_COL = 8


def make_lists(key):
    shape_all = (N_ROW, N_COL, CAP)
    tile_row = lax.broadcasted_iota(jnp.int32, shape_all, 0)
    tile_col = lax.broadcasted_iota(jnp.int32, shape_all, 1)
    slot_id = lax.broadcasted_iota(jnp.int32, shape_all, 2)
    col_pick = jax.random.randint(jax.random.fold_in(key, 11), shape_all, 0, 1048576) % ((tile_row + 1) * SB)
    last_slot = slot_id == CAP - 1
    col_pick = jnp.where(last_slot & (tile_row == N_ROW - 1), N_ROW * SB - 1, col_pick)
    lower_end = jnp.where(col_pick // SB == tile_row, tile_col * SB + col_pick % SB, 0)
    row_pick = lower_end + jax.random.randint(jax.random.fold_in(key, 12), shape_all, 0, 1048576) % (N_COL * SB - lower_end)
    row_pick = jnp.where(last_slot, N_COL * SB - 1, row_pick)
    return (row_pick.astype(jnp.int32), col_pick.astype(jnp.int32))


def draw_row_list(key, part):
    return make_lists(key)[0]


def draw_col_list(key, part):
    return make_lists(key)[1]


def draw_counts(key, part):
    tile_row = lax.broadcasted_iota(jnp.int32, (N_ROW, N_COL), 0)
    base_count = CAP * (tile_row + 1) // N_ROW
    jitter = jax.random.randint(jax.random.fold_in(key, 21), (N_ROW, N_COL), 0, CAP // (2 * N_ROW) + 1)
    result = jnp.where(tile_row == N_ROW - 1, CAP, jnp.maximum(1, base_count - jitter))
    return result.astype(jnp.int32)


def steps_of(own_key, dims, cuts, smallest, top_value):
    factor_of, own = 1.0, jax.random.fold_in(own_key, 6)
    for axis_at, parts in cuts:
        draws = jnp.exp(jax.random.uniform(jax.random.fold_in(own, axis_at), (parts,), jnp.float32, smallest / len(cuts), top_value / len(cuts)))
        factor_of = factor_of * jnp.repeat(draws, dims[axis_at] // parts).reshape([-1 if axis == axis_at else 1 for axis in range(len(dims))])
    return factor_of


def normal_values(rng, dims, width, bound, pieces=(), held_as=jnp.bfloat16):
    values = width * jax.random.normal(rng, dims, jnp.float32)
    if pieces:
        values = values * steps_of(rng, dims, pieces, -0.22, 0.18)
    return jnp.clip(values, -bound, bound).astype(held_as)


def setup_inputs(seed: int = 0) -> dict:
    keys = jax.random.split(jax.random.key(seed), 6)
    return {
        "hamiltonian_blocks": normal_values(keys[0], (N_ROW, N_COL, CAP, BS, BS), (BS * CAP // 4) ** -0.5, 0.0625, ((0, 4), (1, 8)), jnp.float32),
        "block_vectors": normal_values(keys[1], (K, NBASIS), 1.0, 6.0, ((1, 32),), jnp.float32),
        "row_list": draw_row_list(jax.random.fold_in(keys[5], 71), 0),
        "col_list": draw_col_list(jax.random.fold_in(keys[5], 71), 0),
        "counts": draw_counts(jax.random.fold_in(keys[5], 71), 0),
    }


def reference(hamiltonian_blocks, block_vectors, row_list, col_list, counts):
    block_count = N_ROW * N_COL * SB
    tile_total = N_ROW * N_COL
    source = block_vectors.reshape(K, block_count, BS)

    def visit(product_sum, packed):
        blocks, row_slots, col_slots, tile_count, tile_id = packed
        tile_row = tile_id // N_COL
        tile_col = tile_id % N_COL
        global_row = row_slots + tile_row * N_COL * SB
        global_col = (col_slots // SB) * N_COL * SB + tile_col * SB + col_slots % SB
        live_mask = (jnp.arange(CAP, dtype=jnp.int32) < tile_count).astype(jnp.float32)
        col_vectors = source[:, global_col, :]
        row_vectors = source[:, global_row, :]
        direct = jnp.einsum("kpb,pab->kpa", col_vectors, blocks, precision=lax.Precision.HIGHEST) * live_mask[None, :, None]
        mirror = jnp.einsum("kpa,pab->kpb", row_vectors, blocks, precision=lax.Precision.HIGHEST) * live_mask[None, :, None]
        product_sum = product_sum.at[:, global_row, :].add(direct)
        product_sum = product_sum.at[:, global_col, :].add(mirror)
        return product_sum, None

    start_sum = jnp.zeros((K, block_count, BS), jnp.float32)
    packed_all = (
        hamiltonian_blocks.reshape(tile_total, CAP, BS, BS),
        row_list.reshape(tile_total, CAP),
        col_list.reshape(tile_total, CAP),
        counts.reshape(tile_total),
        jnp.arange(tile_total, dtype=jnp.int32),
    )
    product_sum, _ = lax.scan(visit, start_sum, packed_all)
    return product_sum.reshape(K, block_count * BS)
```

```python
import functools

import jax
import jax.numpy as jnp
from jax import lax
from jax.experimental import pallas as pl
from jax.experimental.pallas import tpu as pltpu
from jax.sharding import PartitionSpec as P

SB = 8


def split(x):
    high = x.astype(jnp.bfloat16)
    low = (x - high.astype(jnp.float32)).astype(jnp.bfloat16)
    return high, low


def split_rows(src, dst, vec):
    def body(t, _):
        high, low = split(src[t])
        dst[t, 0:vec, :] = high
        dst[t, vec : 2 * vec, :] = low
        return 0

    lax.fori_loop(0, src.shape[0], body, 0)


def products_kernel(chunk, unroll, rows, cols, counts, blocks, xr, xc, acc_d, acc_m, sr, sc):
    step = pl.program_id(0)
    vec = xr.shape[1]
    width = xr.shape[2]

    @pl.when(step == 0)
    def _():
        acc_d[...] = jnp.zeros_like(acc_d)
        acc_m[...] = jnp.zeros_like(acc_m)
        split_rows(xr, sr, vec)
        split_rows(xc, sc, vec)

    live = counts[0]

    def group(g, _):
        results = []
        for u in range(unroll):
            slot = g * unroll + u
            k = step * chunk + slot
            i = rows[k]
            j = cols[k]
            high, low = split(blocks[slot])
            d = lax.dot_general(
                sc[j],
                jnp.concatenate([high, low], axis=0),
                (((1,), (1,)), ((), ())),
                preferred_element_type=jnp.float32,
            )
            m = lax.dot_general(
                sr[i],
                jnp.concatenate([high, low], axis=1),
                (((1,), (0,)), ((), ())),
                preferred_element_type=jnp.float32,
            )
            mask = jnp.where(k < live, 1.0, 0.0).astype(jnp.float32)
            fold = [
                (z[0:vec, 0:width] + (z[vec : 2 * vec, 0:width] + z[0:vec, width:])) * mask for z in (d, m)
            ]
            results.append((i, j, fold[0], fold[1]))
        for i, j, d, m in results:
            acc_d[i] = acc_d[i] + d
            acc_m[j] = acc_m[j] + m
        return 0

    groups = jnp.clip(pl.cdiv(live - step * chunk, unroll), 0, chunk // unroll)
    lax.fori_loop(0, groups, group, 0)


def products(blocks, xr, xc, rows, cols, counts):
    cap, width, _ = blocks.shape
    vec = xr.shape[1]
    chunk = 32 if cap % 32 == 0 else cap
    unroll = 8 if chunk % 8 == 0 else 1
    whole = lambda shape: pl.BlockSpec(shape, lambda s, *_: (0, 0, 0))
    return pl.pallas_call(
        functools.partial(products_kernel, chunk, unroll),
        grid_spec=pltpu.PrefetchScalarGridSpec(
            num_scalar_prefetch=3,
            grid=(cap // chunk,),
            in_specs=[
                pl.BlockSpec((chunk, width, width), lambda s, *_: (s, 0, 0)),
                whole(xr.shape),
                whole(xc.shape),
            ],
            out_specs=[whole(xr.shape), whole(xc.shape)],
            scratch_shapes=[
                pltpu.VMEM((xr.shape[0], 2 * vec, width), jnp.bfloat16),
                pltpu.VMEM((xc.shape[0], 2 * vec, width), jnp.bfloat16),
            ],
        ),
        out_shape=[
            jax.ShapeDtypeStruct(xr.shape, jnp.float32),
            jax.ShapeDtypeStruct(xc.shape, jnp.float32),
        ],
        compiler_params=pltpu.CompilerParams(vmem_limit_bytes=40 * 2**20),
    )(rows, cols, counts, blocks, xr, xc)


def local(hamiltonian_blocks, block_vectors, row_list, col_list, counts):
    blocks = hamiltonian_blocks[0, 0]
    vec, states = block_vectors.shape
    width = blocks.shape[1]
    own = block_vectors.reshape(vec, SB, width).transpose(1, 0, 2)
    xr = lax.all_gather(own, "col", axis=0, tiled=True)
    xc = lax.all_gather(own, "row", axis=0, tiled=True)
    direct, mirror = products(blocks, xr, xc, row_list[0, 0], col_list[0, 0], counts[0])
    total = lax.psum_scatter(direct, "col", scatter_dimension=0, tiled=True)
    total = total + lax.psum_scatter(mirror, "row", scatter_dimension=0, tiled=True)
    return total.transpose(1, 0, 2).reshape(vec, states)


def solution(mesh):
    return jax.shard_map(
        local,
        mesh=mesh,
        in_specs=(
            P("row", "col", None, None, None),
            P(None, ("row", "col")),
            P("row", "col", None),
            P("row", "col", None),
            P("row", "col"),
        ),
        out_specs=P(None, ("row", "col")),
        check_vma=False,
    )
```

```python
import functools

import jax
import jax.numpy as jnp
from jax import lax
from jax.experimental import pallas as pl
from jax.experimental.pallas import tpu as pltpu
from jax.sharding import PartitionSpec as P

SB = 8


def split(x):
    high = x.astype(jnp.bfloat16)
    low = (x - high.astype(jnp.float32)).astype(jnp.bfloat16)
    return high, low


def split_rows(src, dst, vec):
    def body(t, _):
        high, low = split(src[t])
        dst[t, 0:vec, :] = high
        dst[t, vec : 2 * vec, :] = low
        return 0

    lax.fori_loop(0, src.shape[0], body, 0)


def products_kernel(chunk, unroll, rows, cols, counts, blocks, xr, xc, acc_d, acc_m, sr, sc):
    step = pl.program_id(0)
    vec = xr.shape[1]
    width = xr.shape[2]

    @pl.when(step == 0)
    def _():
        acc_d[...] = jnp.zeros_like(acc_d)
        acc_m[...] = jnp.zeros_like(acc_m)
        split_rows(xr, sr, vec)
        split_rows(xc, sc, vec)

    live = counts[0]

    def group(g, _):
        results = []
        for u in range(unroll):
            slot = g * unroll + u
            k = step * chunk + slot
            i = rows[k]
            j = cols[k]
            high, low = split(blocks[slot])
            d = lax.dot_general(
                sc[j],
                jnp.concatenate([high, low], axis=0),
                (((1,), (1,)), ((), ())),
                preferred_element_type=jnp.float32,
            )
            m = lax.dot_general(
                sr[i],
                jnp.concatenate([high, low], axis=1),
                (((1,), (0,)), ((), ())),
                preferred_element_type=jnp.float32,
            )
            mask = jnp.where(k < live, 1.0, 0.0).astype(jnp.float32)
            fold = [
                (z[0:vec, 0:width] + (z[vec : 2 * vec, 0:width] + z[0:vec, width:])) * mask for z in (d, m)
            ]
            results.append((i, j, fold[0], fold[1]))
        for i, j, d, m in results:
            acc_d[i] = acc_d[i] + d
            acc_m[j] = acc_m[j] + m
        return 0

    groups = jnp.clip(pl.cdiv(live - step * chunk, unroll), 0, chunk // unroll)
    lax.fori_loop(0, groups, group, 0)


def products(blocks, xr, xc, rows, cols, counts):
    cap, width, _ = blocks.shape
    vec = xr.shape[1]
    chunk = 32 if cap % 32 == 0 else cap
    unroll = 8 if chunk % 8 == 0 else 1
    whole = lambda shape: pl.BlockSpec(shape, lambda s, *_: (0, 0, 0))
    return pl.pallas_call(
        functools.partial(products_kernel, chunk, unroll),
        grid_spec=pltpu.PrefetchScalarGridSpec(
            num_scalar_prefetch=3,
            grid=(cap // chunk,),
            in_specs=[
                pl.BlockSpec((chunk, width, width), lambda s, *_: (s, 0, 0)),
                whole(xr.shape),
                whole(xc.shape),
            ],
            out_specs=[whole(xr.shape), whole(xc.shape)],
            scratch_shapes=[
                pltpu.VMEM((xr.shape[0], 2 * vec, width), jnp.bfloat16),
                pltpu.VMEM((xc.shape[0], 2 * vec, width), jnp.bfloat16),
            ],
        ),
        out_shape=[
            jax.ShapeDtypeStruct(xr.shape, jnp.float32),
            jax.ShapeDtypeStruct(xc.shape, jnp.float32),
        ],
        compiler_params=pltpu.CompilerParams(vmem_limit_bytes=40 * 2**20),
    )(rows, cols, counts, blocks, xr, xc)


MESH = pl.DeviceIdType.MESH


def places(n_row, n_col):
    r = lax.axis_index("row")
    c = lax.axis_index("col")
    inner = 2 if n_col % 2 == 0 else 1
    return r, c, c // inner, c % inner, inner, n_col // inner


def greet(n_row, n_col):
    r, c, hi, lo, inner, outer = places(n_row, n_col)
    barrier = pltpu.get_barrier_semaphore()
    met = 0
    for d in range(1, n_row):
        pl.semaphore_signal(barrier, inc=1, device_id=(lax.rem(r + d, n_row), c), device_id_type=MESH)
        met += 1
    for d in range(1, outer):
        pl.semaphore_signal(
            barrier, inc=1, device_id=(r, lax.rem(hi + d, outer) * inner + lo), device_id_type=MESH
        )
        met += 1
    for e in range(1, inner):
        pl.semaphore_signal(
            barrier, inc=1, device_id=(r, hi * inner + lax.rem(lo + e, inner)), device_id_type=MESH
        )
        met += 1
    pl.semaphore_wait(barrier, met)


def remote(src, dst, send, recv, device):
    return pltpu.make_async_remote_copy(
        src_ref=src, dst_ref=dst, send_sem=send, recv_sem=recv, device_id=device, device_id_type=MESH
    )


def gather_kernel(n_row, n_col, vectors, xr, xc, own, z_s, z_r, y_s, y_r, r_s, r_r):
    r, c, hi, lo, inner, outer = places(n_row, n_col)
    width = own.shape[2]
    for t in range(SB):
        own[t] = vectors[:, t * width : (t + 1) * width]
    greet(n_row, n_col)
    mate = hi * inner + (inner - 1 - lo)
    piece = lambda ref, q: ref.at[pl.ds(q * SB, SB)]
    started = []

    def start(*a):
        copy = remote(*a)
        copy.start()
        started.append(copy)

    for d in range(1, outer):
        start(own, piece(xr, c), z_s.at[d], z_r.at[d], (r, lax.rem(hi + d, outer) * inner + lo))
    if inner == 2:
        start(own, piece(xr, c), y_s.at[0], y_r.at[0], (r, mate))
    for d in range(1, n_row):
        start(own, piece(xc, r), r_s.at[d], r_r.at[d], (lax.rem(r + d, n_row), c))
    xr[pl.ds(c * SB, SB)] = own[...]
    xc[pl.ds(r * SB, SB)] = own[...]
    for d in range(1, outer):
        source = piece(xr, lax.rem(hi - d + outer, outer) * inner + lo)
        remote(source, source, z_s.at[d], z_r.at[d], (r, mate)).wait_recv()
        if inner == 2:
            start(source, source, y_s.at[d], y_r.at[d], (r, mate))
    if inner == 2:
        for d in range(outer):
            source = piece(xr, lax.rem(hi - d + outer, outer) * inner + 1 - lo)
            remote(source, source, y_s.at[d], y_r.at[d], (r, mate)).wait_recv()
    for d in range(1, n_row):
        source = piece(xc, lax.rem(r - d + n_row, n_row))
        remote(source, source, r_s.at[d], r_r.at[d], (lax.rem(r + d, n_row), c)).wait_recv()
    for copy in started:
        copy.wait_send()


def scatter_kernel(n_row, n_col, direct, mirror, out, y_buf, z_out, z_buf, r_buf, z_s, z_r, y_s, y_r, r_s, r_r):
    r, c, hi, lo, inner, outer = places(n_row, n_col)
    width = direct.shape[2]
    greet(n_row, n_col)
    mate = hi * inner + (inner - 1 - lo)
    started = []

    def start(*a):
        copy = remote(*a)
        copy.start()
        started.append(copy)
        return copy

    part = lambda ref, q: ref.at[pl.ds(q * SB, SB)]
    to_mate = {}
    order = list(range(1, outer)) + [0]
    if inner == 2:
        for d in order:
            q = lax.rem(hi + d, outer) * inner + 1 - lo
            to_mate[d] = start(part(direct, q), y_buf.at[d], y_s.at[d], y_r.at[d], (r, mate))
    across = [
        start(part(mirror, lax.rem(r + d, n_row)), r_buf.at[d], r_s.at[d], r_r.at[d], (lax.rem(r + d, n_row), c))
        for d in range(1, n_row)
    ]
    along = []
    for d in range(1, outer):
        q = lax.rem(hi + d, outer) * inner + lo
        mine = direct[pl.ds(q * SB, SB)]
        if inner == 2:
            to_mate[d].wait_recv()
            mine = mine + y_buf[d]
        z_out[d] = mine
        along.append(start(z_out.at[d], z_buf.at[d], z_s.at[d], z_r.at[d], (r, q)))
    total = direct[pl.ds(c * SB, SB)] + mirror[pl.ds(r * SB, SB)]
    for d in range(1, n_row):
        across[d - 1].wait_recv()
        total = total + r_buf[d]
    if inner == 2:
        to_mate[0].wait_recv()
        total = total + y_buf[0]
    for d in range(1, outer):
        along[d - 1].wait_recv()
        total = total + z_buf[d]
    for t in range(SB):
        out[:, t * width : (t + 1) * width] = total[t]
    for copy in started:
        copy.wait_send()


def semaphores(n_row, n_col):
    outer = n_col // 2 if n_col % 2 == 0 else n_col
    return [pltpu.SemaphoreType.DMA((n,)) for n in (outer, outer, outer, outer, n_row, n_row)]


def in_vmem(n):
    return [pl.BlockSpec(memory_space=pltpu.VMEM)] * n


def gather(vectors, n_row, n_col, width):
    vec = vectors.shape[0]
    return pl.pallas_call(
        functools.partial(gather_kernel, n_row, n_col),
        out_shape=[jax.ShapeDtypeStruct((n * SB, vec, width), jnp.float32) for n in (n_col, n_row)],
        in_specs=in_vmem(1),
        out_specs=in_vmem(2),
        scratch_shapes=[pltpu.VMEM((SB, vec, width), jnp.float32)] + semaphores(n_row, n_col),
        compiler_params=pltpu.CompilerParams(
            collective_id=0, has_side_effects=True, vmem_limit_bytes=16 * 2**20
        ),
    )(vectors)


def scatter(direct, mirror, n_row, n_col):
    _, vec, width = direct.shape
    outer = n_col // 2 if n_col % 2 == 0 else n_col
    slots = [pltpu.VMEM((n, SB, vec, width), jnp.float32) for n in (outer, outer, outer, n_row)]
    return pl.pallas_call(
        functools.partial(scatter_kernel, n_row, n_col),
        out_shape=jax.ShapeDtypeStruct((vec, SB * width), jnp.float32),
        in_specs=in_vmem(2),
        out_specs=in_vmem(1)[0],
        scratch_shapes=slots + semaphores(n_row, n_col),
        compiler_params=pltpu.CompilerParams(
            collective_id=1, has_side_effects=True, vmem_limit_bytes=16 * 2**20
        ),
    )(direct, mirror)


def local(hamiltonian_blocks, block_vectors, row_list, col_list, counts):
    blocks = hamiltonian_blocks[0, 0]
    n_row = lax.axis_size("row")
    n_col = lax.axis_size("col")
    xr, xc = gather(block_vectors, n_row, n_col, blocks.shape[1])
    direct, mirror = products(blocks, xr, xc, row_list[0, 0], col_list[0, 0], counts[0])
    return scatter(direct, mirror, n_row, n_col)


def solution(mesh):
    return jax.shard_map(
        local,
        mesh=mesh,
        in_specs=(
            P("row", "col", None, None, None),
            P(None, ("row", "col")),
            P("row", "col", None),
            P("row", "col", None),
            P("row", "col"),
        ),
        out_specs=P(None, ("row", "col")),
        check_vma=False,
    )
```

```python
import functools

import jax
import jax.numpy as jnp
from jax import lax
from jax.experimental import pallas as pl
from jax.experimental.pallas import tpu as pltpu
from jax.sharding import PartitionSpec as P

SB = 8


def split(x):
    high = x.astype(jnp.bfloat16)
    low = (x - high.astype(jnp.float32)).astype(jnp.bfloat16)
    return high, low


def split_rows(src, dst, vec):
    def body(t, _):
        high, low = split(src[t])
        dst[t, 0:vec, :] = high
        dst[t, vec : 2 * vec, :] = low
        return 0

    lax.fori_loop(0, src.shape[0], body, 0)


def products_kernel(group, rows, cols, counts, blocks, xr, xc, acc_d, acc_m, sr, sc, held, arrived):
    vec = xr.shape[1]
    width = xr.shape[2]
    steps = held.shape[0] // group

    def fetch(g):
        part = pl.ds(g * group, group)
        return pltpu.make_async_copy(blocks.at[part], held.at[part], arrived.at[g])

    for g in range(steps):
        fetch(g).start()
    acc_d[...] = jnp.zeros_like(acc_d)
    acc_m[...] = jnp.zeros_like(acc_m)
    split_rows(xr, sr, vec)
    split_rows(xc, sc, vec)
    live = counts[0, 0]

    def work(g):
        results = []
        for u in range(group):
            k = g * group + u
            i = rows[0, 0, k]
            j = cols[0, 0, k]
            high, low = split(held[k])
            d = lax.dot_general(
                sc[j],
                jnp.concatenate([high, low], axis=0),
                (((1,), (1,)), ((), ())),
                preferred_element_type=jnp.float32,
            )
            m = lax.dot_general(
                sr[i],
                jnp.concatenate([high, low], axis=1),
                (((1,), (0,)), ((), ())),
                preferred_element_type=jnp.float32,
            )
            mask = jnp.where(k < live, 1.0, 0.0).astype(jnp.float32)
            fold = [
                (z[0:vec, 0:width] + (z[vec : 2 * vec, 0:width] + z[0:vec, width:])) * mask for z in (d, m)
            ]
            results.append((i, j, fold[0], fold[1]))
        for i, j, d, m in results:
            acc_d[i] = acc_d[i] + d
            acc_m[j] = acc_m[j] + m

    def step(g, _):
        fetch(g).wait()
        pl.when(g * group < live)(lambda: work(g))
        return 0

    lax.fori_loop(0, steps, step, 0)


def products(blocks, xr, xc, rows, cols, counts):
    cap, width, _ = blocks.shape
    vec = xr.shape[1]
    group = next(n for n in (16, 8, 4, 2, 1) if cap % n == 0)
    return pl.pallas_call(
        functools.partial(products_kernel, group),
        in_specs=[pl.BlockSpec(memory_space=pltpu.SMEM)] * 3
        + [pl.BlockSpec(memory_space=pl.ANY)]
        + in_vmem(2),
        out_specs=in_vmem(2),
        out_shape=[
            jax.ShapeDtypeStruct(xr.shape, jnp.float32),
            jax.ShapeDtypeStruct(xc.shape, jnp.float32),
        ],
        scratch_shapes=[
            pltpu.VMEM((xr.shape[0], 2 * vec, width), jnp.bfloat16),
            pltpu.VMEM((xc.shape[0], 2 * vec, width), jnp.bfloat16),
            pltpu.VMEM(blocks.shape, jnp.float32),
            pltpu.SemaphoreType.DMA((cap // group,)),
        ],
        compiler_params=pltpu.CompilerParams(vmem_limit_bytes=48 * 2**20),
    )(rows, cols, counts, blocks, xr, xc)


MESH = pl.DeviceIdType.MESH


def places(n_row, n_col):
    r = lax.axis_index("row")
    c = lax.axis_index("col")
    inner = 2 if n_col % 2 == 0 else 1
    return r, c, c // inner, c % inner, inner, n_col // inner


def greet(n_row, n_col):
    r, c, hi, lo, inner, outer = places(n_row, n_col)
    barrier = pltpu.get_barrier_semaphore()
    met = 0
    for d in range(1, n_row):
        pl.semaphore_signal(barrier, inc=1, device_id=(lax.rem(r + d, n_row), c), device_id_type=MESH)
        met += 1
    for d in range(1, outer):
        pl.semaphore_signal(
            barrier, inc=1, device_id=(r, lax.rem(hi + d, outer) * inner + lo), device_id_type=MESH
        )
        met += 1
    for e in range(1, inner):
        pl.semaphore_signal(
            barrier, inc=1, device_id=(r, hi * inner + lax.rem(lo + e, inner)), device_id_type=MESH
        )
        met += 1
    pl.semaphore_wait(barrier, met)


def remote(src, dst, send, recv, device):
    return pltpu.make_async_remote_copy(
        src_ref=src, dst_ref=dst, send_sem=send, recv_sem=recv, device_id=device, device_id_type=MESH
    )


def gather_kernel(n_row, n_col, vectors, xr, xc, own, z_s, z_r, y_s, y_r, r_s, r_r):
    r, c, hi, lo, inner, outer = places(n_row, n_col)
    width = own.shape[2]
    for t in range(SB):
        own[t] = vectors[:, t * width : (t + 1) * width]
    greet(n_row, n_col)
    mate = hi * inner + (inner - 1 - lo)
    piece = lambda ref, q: ref.at[pl.ds(q * SB, SB)]
    started = []

    def start(*a):
        copy = remote(*a)
        copy.start()
        started.append(copy)

    for d in range(1, outer):
        start(own, piece(xr, c), z_s.at[d], z_r.at[d], (r, lax.rem(hi + d, outer) * inner + lo))
    if inner == 2:
        start(own, piece(xr, c), y_s.at[0], y_r.at[0], (r, mate))
    for d in range(1, n_row):
        start(own, piece(xc, r), r_s.at[d], r_r.at[d], (lax.rem(r + d, n_row), c))
    xr[pl.ds(c * SB, SB)] = own[...]
    xc[pl.ds(r * SB, SB)] = own[...]
    for d in range(1, outer):
        source = piece(xr, lax.rem(hi - d + outer, outer) * inner + lo)
        remote(source, source, z_s.at[d], z_r.at[d], (r, mate)).wait_recv()
        if inner == 2:
            start(source, source, y_s.at[d], y_r.at[d], (r, mate))
    if inner == 2:
        for d in range(outer):
            source = piece(xr, lax.rem(hi - d + outer, outer) * inner + 1 - lo)
            remote(source, source, y_s.at[d], y_r.at[d], (r, mate)).wait_recv()
    for d in range(1, n_row):
        source = piece(xc, lax.rem(r - d + n_row, n_row))
        remote(source, source, r_s.at[d], r_r.at[d], (lax.rem(r + d, n_row), c)).wait_recv()
    for copy in started:
        copy.wait_send()


def scatter_kernel(n_row, n_col, direct, mirror, out, y_buf, z_out, z_buf, r_buf, z_s, z_r, y_s, y_r, r_s, r_r):
    r, c, hi, lo, inner, outer = places(n_row, n_col)
    width = direct.shape[2]
    greet(n_row, n_col)
    mate = hi * inner + (inner - 1 - lo)
    started = []

    def start(*a):
        copy = remote(*a)
        copy.start()
        started.append(copy)
        return copy

    part = lambda ref, q: ref.at[pl.ds(q * SB, SB)]
    to_mate = {}
    order = list(range(1, outer)) + [0]
    if inner == 2:
        for d in order:
            q = lax.rem(hi + d, outer) * inner + 1 - lo
            to_mate[d] = start(part(direct, q), y_buf.at[d], y_s.at[d], y_r.at[d], (r, mate))
    across = [
        start(part(mirror, lax.rem(r + d, n_row)), r_buf.at[d], r_s.at[d], r_r.at[d], (lax.rem(r + d, n_row), c))
        for d in range(1, n_row)
    ]
    along = []
    for d in range(1, outer):
        q = lax.rem(hi + d, outer) * inner + lo
        mine = direct[pl.ds(q * SB, SB)]
        if inner == 2:
            to_mate[d].wait_recv()
            mine = mine + y_buf[d]
        z_out[d] = mine
        along.append(start(z_out.at[d], z_buf.at[d], z_s.at[d], z_r.at[d], (r, q)))
    total = direct[pl.ds(c * SB, SB)] + mirror[pl.ds(r * SB, SB)]
    for d in range(1, n_row):
        across[d - 1].wait_recv()
        total = total + r_buf[d]
    if inner == 2:
        to_mate[0].wait_recv()
        total = total + y_buf[0]
    for d in range(1, outer):
        along[d - 1].wait_recv()
        total = total + z_buf[d]
    for t in range(SB):
        out[:, t * width : (t + 1) * width] = total[t]
    for copy in started:
        copy.wait_send()


def semaphores(n_row, n_col):
    outer = n_col // 2 if n_col % 2 == 0 else n_col
    return [pltpu.SemaphoreType.DMA((n,)) for n in (outer, outer, outer, outer, n_row, n_row)]


def in_vmem(n):
    return [pl.BlockSpec(memory_space=pltpu.VMEM)] * n


def gather(vectors, n_row, n_col, width):
    vec = vectors.shape[0]
    return pl.pallas_call(
        functools.partial(gather_kernel, n_row, n_col),
        out_shape=[jax.ShapeDtypeStruct((n * SB, vec, width), jnp.float32) for n in (n_col, n_row)],
        in_specs=in_vmem(1),
        out_specs=in_vmem(2),
        scratch_shapes=[pltpu.VMEM((SB, vec, width), jnp.float32)] + semaphores(n_row, n_col),
        compiler_params=pltpu.CompilerParams(
            collective_id=0, has_side_effects=True, vmem_limit_bytes=16 * 2**20
        ),
    )(vectors)


def scatter(direct, mirror, n_row, n_col):
    _, vec, width = direct.shape
    outer = n_col // 2 if n_col % 2 == 0 else n_col
    slots = [pltpu.VMEM((n, SB, vec, width), jnp.float32) for n in (outer, outer, outer, n_row)]
    return pl.pallas_call(
        functools.partial(scatter_kernel, n_row, n_col),
        out_shape=jax.ShapeDtypeStruct((vec, SB * width), jnp.float32),
        in_specs=in_vmem(2),
        out_specs=in_vmem(1)[0],
        scratch_shapes=slots + semaphores(n_row, n_col),
        compiler_params=pltpu.CompilerParams(
            collective_id=1, has_side_effects=True, vmem_limit_bytes=16 * 2**20
        ),
    )(direct, mirror)


def local(hamiltonian_blocks, block_vectors, row_list, col_list, counts):
    blocks = hamiltonian_blocks[0, 0]
    n_row = lax.axis_size("row")
    n_col = lax.axis_size("col")
    xr, xc = gather(block_vectors, n_row, n_col, blocks.shape[1])
    direct, mirror = products(blocks, xr, xc, row_list, col_list, counts)
    return scatter(direct, mirror, n_row, n_col)


def solution(mesh):
    return jax.shard_map(
        local,
        mesh=mesh,
        in_specs=(
            P("row", "col", None, None, None),
            P(None, ("row", "col")),
            P("row", "col", None),
            P("row", "col", None),
            P("row", "col"),
        ),
        out_specs=P(None, ("row", "col")),
        check_vma=False,
    )
```

```python
import functools

import jax
import jax.numpy as jnp
from jax import lax
from jax.experimental import pallas as pl
from jax.experimental.pallas import tpu as pltpu
from jax.sharding import PartitionSpec as P

SB = 8


def split(x):
    high = x.astype(jnp.bfloat16)
    low = (x - high.astype(jnp.float32)).astype(jnp.bfloat16)
    return high, low


def split_rows(src, dst, vec):
    def body(t, _):
        high, low = split(src[t])
        dst[t, 0:vec, :] = high
        dst[t, vec : 2 * vec, :] = low
        return 0

    lax.fori_loop(0, src.shape[0], body, 0, unroll=8)


def products_kernel(group, rows, cols, counts, blocks, xr, xc, acc_d, acc_m, sr, sc, held, arrived):
    vec = xr.shape[1]
    width = xr.shape[2]
    steps = held.shape[0] // group

    def fetch(g):
        part = pl.ds(g * group, group)
        return pltpu.make_async_copy(blocks.at[part], held.at[part], arrived.at[g])

    for g in range(steps):
        fetch(g).start()
    acc_d[...] = jnp.zeros_like(acc_d)
    acc_m[...] = jnp.zeros_like(acc_m)
    split_rows(xr, sr, vec)
    split_rows(xc, sc, vec)
    live = counts[0, 0]

    def work(g):
        results = []
        for u in range(group):
            k = g * group + u
            i = rows[0, 0, k]
            j = cols[0, 0, k]
            high, low = split(held[k])
            d = lax.dot_general(
                sc[j],
                jnp.concatenate([high, low], axis=0),
                (((1,), (1,)), ((), ())),
                preferred_element_type=jnp.float32,
            )
            m = lax.dot_general(
                sr[i],
                jnp.concatenate([high, low], axis=1),
                (((1,), (0,)), ((), ())),
                preferred_element_type=jnp.float32,
            )
            mask = jnp.where(k < live, 1.0, 0.0).astype(jnp.float32)
            fold = [
                (z[0:vec, 0:width] + (z[vec : 2 * vec, 0:width] + z[0:vec, width:])) * mask for z in (d, m)
            ]
            results.append((i, j, fold[0], fold[1]))
        for i, j, d, m in results:
            acc_d[i] = acc_d[i] + d
            acc_m[j] = acc_m[j] + m

    def step(g, _):
        fetch(g).wait()
        pl.when(g * group < live)(lambda: work(g))
        return 0

    lax.fori_loop(0, steps, step, 0)


def products(blocks, xr, xc, rows, cols, counts):
    cap, width, _ = blocks.shape
    vec = xr.shape[1]
    group = next(n for n in (16, 8, 4, 2, 1) if cap % n == 0)
    return pl.pallas_call(
        functools.partial(products_kernel, group),
        in_specs=[pl.BlockSpec(memory_space=pltpu.SMEM)] * 3
        + [pl.BlockSpec(memory_space=pl.ANY)]
        + in_vmem(2),
        out_specs=in_vmem(2),
        out_shape=[
            jax.ShapeDtypeStruct(xr.shape, jnp.float32),
            jax.ShapeDtypeStruct(xc.shape, jnp.float32),
        ],
        scratch_shapes=[
            pltpu.VMEM((xr.shape[0], 2 * vec, width), jnp.bfloat16),
            pltpu.VMEM((xc.shape[0], 2 * vec, width), jnp.bfloat16),
            pltpu.VMEM(blocks.shape, jnp.float32),
            pltpu.SemaphoreType.DMA((cap // group,)),
        ],
        compiler_params=pltpu.CompilerParams(vmem_limit_bytes=48 * 2**20),
    )(rows, cols, counts, blocks, xr, xc)


MESH = pl.DeviceIdType.MESH


def places(n_row, n_col):
    r = lax.axis_index("row")
    c = lax.axis_index("col")
    inner = 2 if n_col % 2 == 0 else 1
    return r, c, c // inner, c % inner, inner, n_col // inner


def greet(n_row, n_col):
    r, c, hi, lo, inner, outer = places(n_row, n_col)
    barrier = pltpu.get_barrier_semaphore()
    met = 0
    for d in range(1, n_row):
        pl.semaphore_signal(barrier, inc=1, device_id=(lax.rem(r + d, n_row), c), device_id_type=MESH)
        met += 1
    for d in range(1, outer):
        pl.semaphore_signal(
            barrier, inc=1, device_id=(r, lax.rem(hi + d, outer) * inner + lo), device_id_type=MESH
        )
        met += 1
    for e in range(1, inner):
        pl.semaphore_signal(
            barrier, inc=1, device_id=(r, hi * inner + lax.rem(lo + e, inner)), device_id_type=MESH
        )
        met += 1
    pl.semaphore_wait(barrier, met)


def remote(src, dst, send, recv, device):
    return pltpu.make_async_remote_copy(
        src_ref=src, dst_ref=dst, send_sem=send, recv_sem=recv, device_id=device, device_id_type=MESH
    )


def gather_kernel(n_row, n_col, vectors, xr, xc, own, z_s, z_r, y_s, y_r, r_s, r_r):
    r, c, hi, lo, inner, outer = places(n_row, n_col)
    width = own.shape[2]
    for t in range(SB):
        own[t] = vectors[:, t * width : (t + 1) * width]
    greet(n_row, n_col)
    mate = hi * inner + (inner - 1 - lo)
    piece = lambda ref, q: ref.at[pl.ds(q * SB, SB)]
    started = []

    def start(*a):
        copy = remote(*a)
        copy.start()
        started.append(copy)

    for d in range(1, outer):
        start(own, piece(xr, c), z_s.at[d], z_r.at[d], (r, lax.rem(hi + d, outer) * inner + lo))
    if inner == 2:
        start(own, piece(xr, c), y_s.at[0], y_r.at[0], (r, mate))
    for d in range(1, n_row):
        start(own, piece(xc, r), r_s.at[d], r_r.at[d], (lax.rem(r + d, n_row), c))
    xr[pl.ds(c * SB, SB)] = own[...]
    xc[pl.ds(r * SB, SB)] = own[...]
    for d in range(1, outer):
        source = piece(xr, lax.rem(hi - d + outer, outer) * inner + lo)
        remote(source, source, z_s.at[d], z_r.at[d], (r, mate)).wait_recv()
        if inner == 2:
            start(source, source, y_s.at[d], y_r.at[d], (r, mate))
    if inner == 2:
        for d in range(outer):
            source = piece(xr, lax.rem(hi - d + outer, outer) * inner + 1 - lo)
            remote(source, source, y_s.at[d], y_r.at[d], (r, mate)).wait_recv()
    for d in range(1, n_row):
        source = piece(xc, lax.rem(r - d + n_row, n_row))
        remote(source, source, r_s.at[d], r_r.at[d], (lax.rem(r + d, n_row), c)).wait_recv()
    for copy in started:
        copy.wait_send()


def scatter_kernel(n_row, n_col, direct, mirror, out, y_buf, z_out, z_buf, r_buf, z_s, z_r, y_s, y_r, r_s, r_r):
    r, c, hi, lo, inner, outer = places(n_row, n_col)
    width = direct.shape[2]
    greet(n_row, n_col)
    mate = hi * inner + (inner - 1 - lo)
    started = []

    def start(*a):
        copy = remote(*a)
        copy.start()
        started.append(copy)
        return copy

    part = lambda ref, q: ref.at[pl.ds(q * SB, SB)]
    to_mate = {}
    order = list(range(1, outer)) + [0]
    if inner == 2:
        for d in order:
            q = lax.rem(hi + d, outer) * inner + 1 - lo
            to_mate[d] = start(part(direct, q), y_buf.at[d], y_s.at[d], y_r.at[d], (r, mate))
    across = [
        start(part(mirror, lax.rem(r + d, n_row)), r_buf.at[d], r_s.at[d], r_r.at[d], (lax.rem(r + d, n_row), c))
        for d in range(1, n_row)
    ]
    along = []
    for d in range(1, outer):
        q = lax.rem(hi + d, outer) * inner + lo
        mine = direct[pl.ds(q * SB, SB)]
        if inner == 2:
            to_mate[d].wait_recv()
            mine = mine + y_buf[d]
        z_out[d] = mine
        along.append(start(z_out.at[d], z_buf.at[d], z_s.at[d], z_r.at[d], (r, q)))
    total = direct[pl.ds(c * SB, SB)] + mirror[pl.ds(r * SB, SB)]
    for d in range(1, n_row):
        across[d - 1].wait_recv()
        total = total + r_buf[d]
    if inner == 2:
        to_mate[0].wait_recv()
        total = total + y_buf[0]
    for d in range(1, outer):
        along[d - 1].wait_recv()
        total = total + z_buf[d]
    for t in range(SB):
        out[:, t * width : (t + 1) * width] = total[t]
    for copy in started:
        copy.wait_send()


def semaphores(n_row, n_col):
    outer = n_col // 2 if n_col % 2 == 0 else n_col
    return [pltpu.SemaphoreType.DMA((n,)) for n in (outer, outer, outer, outer, n_row, n_row)]


def in_vmem(n):
    return [pl.BlockSpec(memory_space=pltpu.VMEM)] * n


def gather(vectors, n_row, n_col, width):
    vec = vectors.shape[0]
    return pl.pallas_call(
        functools.partial(gather_kernel, n_row, n_col),
        out_shape=[jax.ShapeDtypeStruct((n * SB, vec, width), jnp.float32) for n in (n_col, n_row)],
        in_specs=in_vmem(1),
        out_specs=in_vmem(2),
        scratch_shapes=[pltpu.VMEM((SB, vec, width), jnp.float32)] + semaphores(n_row, n_col),
        compiler_params=pltpu.CompilerParams(
            collective_id=0, has_side_effects=True, vmem_limit_bytes=16 * 2**20
        ),
    )(vectors)


def scatter(direct, mirror, n_row, n_col):
    _, vec, width = direct.shape
    outer = n_col // 2 if n_col % 2 == 0 else n_col
    slots = [pltpu.VMEM((n, SB, vec, width), jnp.float32) for n in (outer, outer, outer, n_row)]
    return pl.pallas_call(
        functools.partial(scatter_kernel, n_row, n_col),
        out_shape=jax.ShapeDtypeStruct((vec, SB * width), jnp.float32),
        in_specs=in_vmem(2),
        out_specs=in_vmem(1)[0],
        scratch_shapes=slots + semaphores(n_row, n_col),
        compiler_params=pltpu.CompilerParams(
            collective_id=1, has_side_effects=True, vmem_limit_bytes=16 * 2**20
        ),
    )(direct, mirror)


def local(hamiltonian_blocks, block_vectors, row_list, col_list, counts):
    blocks = hamiltonian_blocks[0, 0]
    n_row = lax.axis_size("row")
    n_col = lax.axis_size("col")
    xr, xc = gather(block_vectors, n_row, n_col, blocks.shape[1])
    direct, mirror = products(blocks, xr, xc, row_list, col_list, counts)
    return scatter(direct, mirror, n_row, n_col)


def solution(mesh):
    return jax.shard_map(
        local,
        mesh=mesh,
        in_specs=(
            P("row", "col", None, None, None),
            P(None, ("row", "col")),
            P("row", "col", None),
            P("row", "col", None),
            P("row", "col"),
        ),
        out_specs=P(None, ("row", "col")),
        check_vma=False,
    )
```
